32 devices in a mesh: replica: 4 (over x, core), fsdp: 8 (over z, y).
Axes of the slice: x: 2, y: 2, z: 4, core: 2. Of those that a mesh axis runs over, the one named last changes fastest.
Arguments:
- hidden_in: bfloat16 [4096, 4096], P(('replica', 'fsdp')), may hold values from -60 to 60
- res_grad: bfloat16 [4096, 4096], P(('replica', 'fsdp')), may hold values from -0.59765625 to 0.59765625
- value_grad: bfloat16 [4096, 512], P(('replica', 'fsdp')), may hold values from -1.5 to 1.5
- value_weight: bfloat16 [4, 4096, 512], P('replica', 'fsdp'), may hold values from -0.09375 to 0.09375
- norm_gain: float32 [4, 4096], P('replica'), may hold values from 0.5 to 1.5
- inner_frag: float32 [4, 4096, 768], P('replica', 'fsdp'), may hold values from -6 to 6
- outer_frag: float32 [4096, 768], P('fsdp'), may hold values from -6 to 6
- momentum: float32 [4096, 768], P('fsdp'), may hold values from -3 to 3
Outputs:
- hidden_grad: bfloat16 [4096, 4096], P(('replica', 'fsdp'))
- weight_grad: bfloat16 [4, 4096, 512], P('replica', 'fsdp')
- gain_grad: float32 [4, 4096], P('replica', 'fsdp')
- new_outer: float32 [4096, 768], P('fsdp')
- new_momentum: float32 [4096, 768], P('fsdp')
The draws below stay inside these ranges and needn't reach their ends.
All inputs are finite; a program needn't handle non-finite values.
Results may differ from the reference program's by a relative error of at most 0.015.
Values may be sent and summed in bfloat16 or wider, within the bound.
A program may use at most 64 MiB of HBM per device.

```python
import math
import jax
import jax.numpy as jnp
from jax import lax

D = 4096
KVW = 512
FW = 768
TOK_DEV = 128
TOKENS = 4096
N_REPLICA = 4
N_FSDP = 8


def draw_hidden_in(key, part):
    first_key = jax.random.fold_in(key, 11)
    second_key = jax.random.fold_in(key, 12)
    column_scale = jnp.exp(jax.random.uniform(second_key, (D,), jnp.float32, 0.0, math.log(10.0)))
    base_values = jnp.clip(jax.random.normal(first_key, (TOKENS, D), jnp.float32), -6.0, 6.0)
    values = base_values * column_scale
    return values.astype(jnp.bfloat16)


def level_of(rng, dims, shards, least, high):
    factor_of, own = 1.0, jax.random.fold_in(rng, 6)
    for axis_at, shards_of in shards:
        draws = jnp.exp(jax.random.uniform(jax.random.fold_in(own, axis_at), (shards_of,), jnp.float32, least / len(shards), high / len(shards)))
        factor_of = factor_of * jnp.repeat(draws, dims[axis_at] // shards_of).reshape([-1 if axis == axis_at else 1 for axis in range(len(dims))])
    return factor_of


def scatter_about(rng, shape, spread, reach, pieces=(), dtype=jnp.bfloat16):
    gain = level_of(rng, shape, pieces, -0.22, 0.18) if pieces else 1.0
    entries = jax.random.normal(rng, shape, jnp.float32) * spread * gain
    return jnp.minimum(jnp.maximum(entries, -reach), reach).astype(dtype)


def setup_inputs(seed: int = 0) -> dict:
    key_of = jax.random.split(jax.random.key(seed), 9)
    hidden_in = draw_hidden_in(jax.random.fold_in(key_of[8], 71), 0)
    res_grad = scatter_about(key_of[1], (TOKENS, D), 0.1, 0.59765625, ((0, 32),))
    value_grad = scatter_about(key_of[2], (TOKENS, KVW), 0.25, 1.5, ((0, 32),))
    value_weight = scatter_about(key_of[3], (N_REPLICA, D, KVW), D ** -0.5, 0.09375, ((0, 4), (1, 8)))
    norm_gain = jnp.clip(1.0 + 0.1 * jax.random.normal(key_of[4], (N_REPLICA, D), jnp.float32), 0.5, 1.5)
    inner_frag = scatter_about(key_of[5], (N_REPLICA, D, FW), 1.0, 6.0, ((0, 4), (1, 8)), jnp.float32)
    outer_frag = scatter_about(key_of[6], (D, FW), 1.0, 6.0, ((0, 8),), jnp.float32)
    momentum = scatter_about(key_of[7], (D, FW), 0.5, 3.0, ((0, 8),), jnp.float32)
    return {"hidden_in": hidden_in, "res_grad": res_grad, "value_grad": value_grad, "value_weight": value_weight, "norm_gain": norm_gain, "inner_frag": inner_frag, "outer_frag": outer_frag, "momentum": momentum}


def replica_backward(operands):
    hidden_rows, res_rows, value_rows, weight, scales = operands
    widened = hidden_rows.astype(jnp.float32)
    inverse = lax.rsqrt(lax.optimization_barrier(jnp.mean(widened * widened, axis=1, keepdims=True)) + 1e-05)
    unit_rows = widened * inverse
    normed = (unit_rows * scales).astype(jnp.bfloat16)
    input_grad = jnp.dot(value_rows, weight.T, preferred_element_type=jnp.float32)
    gain_grad = lax.optimization_barrier(jnp.sum(input_grad * unit_rows, axis=0))
    scaled = input_grad * scales
    projection = lax.optimization_barrier(jnp.mean(scaled * unit_rows, axis=1, keepdims=True))
    hidden_grad = (res_rows.astype(jnp.float32) + inverse * (scaled - unit_rows * projection)).astype(jnp.bfloat16)
    groups_normed = normed.reshape(N_FSDP, TOK_DEV, D)
    groups_value = value_rows.reshape(N_FSDP, TOK_DEV, KVW)

    def add_group(carry, paired):
        product = jnp.dot(paired[0].T, paired[1], preferred_element_type=jnp.float32)
        rounded = lax.optimization_barrier(product.astype(jnp.bfloat16))
        return (carry + rounded.astype(jnp.float32), None)
    weight_grad, _ = lax.scan(add_group, jnp.zeros((D, KVW), jnp.float32), (groups_normed, groups_value))
    return (hidden_grad, weight_grad.astype(jnp.bfloat16), gain_grad)

def reference(hidden_in, res_grad, value_grad, value_weight, norm_gain, inner_frag, outer_frag, momentum):
    hidden_grad, weight_grad, gain_grad = lax.map(replica_backward, (hidden_in.reshape(N_REPLICA, N_FSDP * TOK_DEV, D), res_grad.reshape(N_REPLICA, N_FSDP * TOK_DEV, D), value_grad.reshape(N_REPLICA, N_FSDP * TOK_DEV, KVW), value_weight, norm_gain))
    hidden_grad = hidden_grad.reshape(TOKENS, D)

    def add_replica(carry, frag):
        return (carry + (outer_frag - frag), None)
    summed, _ = lax.scan(add_replica, jnp.zeros((D, FW), jnp.float32), inner_frag)
    average = summed / N_REPLICA
    new_momentum = 0.9 * momentum + average
    new_outer = outer_frag - 0.7 * (average + 0.9 * new_momentum)
    return (hidden_grad, weight_grad, gain_grad, new_outer, new_momentum)
```

```python
import functools

import jax
import jax.numpy as jnp
from jax import lax
from jax.experimental import pallas as pl
from jax.experimental.pallas import tpu as pltpu
from jax.sharding import PartitionSpec as P

MESH = pl.DeviceIdType.MESH
F32 = jnp.float32
BF16 = jnp.bfloat16
EPS = 1e-05


def kernel(
    n, reps, with_frag,
    hid, res_h, vg, w, gain, inner_h, outer_h, mom_h,
    hg_h, wg_out, gg_out, no_h, nm_h,
    inv, nrm_s, nrm_r, vg_r, ig_s, ig_r, wg_acc, res, hg,
    inner, outer, mom, ps, fr_r, av,
    vg_send, vg_recv, nrm_send, nrm_recv, ig_send, ig_recv,
    fr_send, fr_recv, av_send, av_recv, local,
):
    tokens, width = hid.shape
    feats = width // n
    half = n // 2
    me = lax.axis_index("fsdp")
    rep = lax.axis_index("replica")
    zrow, ycol = me // 2, lax.rem(me, 2)
    mirror = (half - 1 - zrow) * 2 + ycol
    base = (me // half) * half
    far = half - base
    mine, theirs = me - base, mirror - far

    def near_peer(j):
        return base + lax.rem(mine + j, half)

    def far_peer(j):
        return far + lax.rem(theirs + j, half)

    def cols(i):
        return pl.ds(pl.multiple_of(i * feats, feats), feats)

    def remote(src, dst, send, recv, dest, axis="fsdp"):
        return pltpu.make_async_remote_copy(
            src_ref=src, dst_ref=dst, send_sem=send, recv_sem=recv,
            device_id={axis: dest}, device_id_type=MESH,
        )

    loads = [pltpu.make_async_copy(res_h, res, local.at[0])]
    if with_frag:
        loads += [
            pltpu.make_async_copy(inner_h, inner, local.at[1]),
            pltpu.make_async_copy(outer_h, outer, local.at[2]),
            pltpu.make_async_copy(mom_h, mom, local.at[3]),
        ]
    for load in loads:
        load.start()

    barrier = pltpu.get_barrier_semaphore()
    for k in range(1, n):
        pl.semaphore_signal(
            barrier, inc=1, device_id={"fsdp": lax.rem(me + k, n)}, device_id_type=MESH
        )
    if with_frag:
        for k in range(1, reps):
            pl.semaphore_signal(
                barrier, inc=1, device_id={"replica": lax.rem(rep + k, reps)}, device_id_type=MESH
            )
    pl.semaphore_wait(barrier, n - 1 + (reps - 1 if with_frag else 0))

    def vg_own(slot, dest):
        return remote(vg, vg_r.at[me], vg_send.at[slot], vg_recv.at[me], dest)

    def vg_forward(j):
        return remote(
            vg_r.at[mirror], vg_r.at[mirror], vg_send.at[half + j], vg_recv.at[mirror], near_peer(j)
        )

    vg_own(0, mirror).start()
    for j in range(1, half):
        vg_own(j, near_peer(j)).start()
    vg_r[me] = vg[...]

    rows = 16

    @pl.loop(0, tokens // rows)
    def _(c):
        at = pl.ds(pl.multiple_of(c * rows, rows), rows)
        total = jnp.zeros((rows, feats), F32)
        for b in range(n):
            x = hid[at, b * feats:(b + 1) * feats].astype(F32)
            total += x * x
        mean = jnp.sum(total, axis=1, keepdims=True) / width
        inv[at, :] = jnp.broadcast_to(lax.rsqrt(mean + EPS), (rows, 128))

    def norm_block(dest, out, slot):
        scale = gain[:, cols(dest)]

        @pl.loop(0, tokens // rows)
        def _(c):
            at = pl.ds(pl.multiple_of(c * rows, rows), rows)
            unit = hid[at, cols(dest)].astype(F32) * inv[at, 0:1]
            out[slot, at, :] = (unit * scale).astype(BF16)

    def nrm_copy(dest):
        return remote(
            nrm_s.at[dest], nrm_r.at[me], nrm_send.at[dest], nrm_recv.at[me], dest
        )

    @pl.loop(0, half)
    def _(j):
        dest = far_peer(j)
        norm_block(dest, nrm_s, dest)
        nrm_copy(dest).start()

    @pl.loop(1, half)
    def _(j):
        dest = near_peer(j)
        norm_block(dest, nrm_s, dest)
        nrm_copy(dest).start()

    norm_block(me, nrm_r, me)

    def fr_copy(k):
        dest = lax.rem(rep + k, reps)
        return remote(
            ps.at[dest], fr_r.at[rep], fr_send.at[dest], fr_recv.at[rep], dest, "replica"
        )

    def av_copy(k):
        dest = lax.rem(rep + k, reps)
        return remote(
            av.at[rep], av.at[rep], av_send.at[dest], av_recv.at[rep], dest, "replica"
        )

    if with_frag:
        share = ps.shape[1]
        steps = share // rows
        for load in loads[1:]:
            load.wait()

        @pl.loop(0, reps * steps)
        def _(c):
            at = pl.ds(pl.multiple_of(c * rows, rows), rows)
            to = pl.ds(pl.multiple_of(lax.rem(c, steps) * rows, rows), rows)
            ps[c // steps, to, :] = (outer[at, :] - inner[at, :]).astype(BF16)

        for k in range(1, reps):
            fr_copy(k).start()

    remote(vg, vg_r.at[mirror], vg_send.at[0], vg_recv.at[mirror], mirror).wait_recv()
    for j in range(1, half):
        vg_forward(j).start()

    def ig_dot(src):
        return lax.dot_general(
            vg_r[src], w[...], (((1,), (1,)), ((), ())), preferred_element_type=F32
        ).astype(BF16)

    def ig_copy(src):
        return remote(ig_s.at[src], ig_r.at[me], ig_send.at[src], ig_recv.at[me], src)

    def vg_wait(src):
        remote(vg, vg_r.at[src], vg_send.at[0], vg_recv.at[src], src).wait_recv()

    ig_s[mirror] = ig_dot(mirror)
    ig_copy(mirror).start()

    @pl.loop(1, half)
    def _(j):
        src = near_peer(j)
        vg_wait(src)
        ig_s[src] = ig_dot(src)
        ig_copy(src).start()

    @pl.loop(1, half)
    def _(j):
        src = far_peer(j)
        vg_wait(src)
        ig_s[src] = ig_dot(src)
        ig_copy(src).start()

    own = ig_dot(me)
    ig_s[me] = own
    ig_r[me] = own

    stores = []
    if with_frag:
        for k in range(1, reps):
            src = lax.rem(rep + k, reps)
            remote(
                ps.at[src], fr_r.at[src], fr_send.at[src], fr_recv.at[src], src, "replica"
            ).wait_recv()
        fr_r[rep] = ps[rep]

        @pl.loop(0, steps)
        def _(c):
            at = pl.ds(pl.multiple_of(c * rows, rows), rows)
            total = fr_r[0, at, :].astype(F32)
            for r in range(1, reps):
                total += fr_r[r, at, :].astype(F32)
            av[rep, at, :] = (total / reps).astype(BF16)

        for k in range(1, reps):
            av_copy(k).start()
        for k in range(1, reps):
            src = lax.rem(rep + k, reps)
            remote(
                av.at[src], av.at[src], av_send.at[src], av_recv.at[src], src, "replica"
            ).wait_recv()

        @pl.loop(0, reps * steps)
        def _(c):
            at = pl.ds(pl.multiple_of(c * rows, rows), rows)
            to = pl.ds(pl.multiple_of(lax.rem(c, steps) * rows, rows), rows)
            average = av[c // steps, to, :].astype(F32)
            momentum = 0.9 * mom[at, :] + average
            mom[at, :] = momentum
            outer[at, :] = outer[at, :] - 0.7 * (average + 0.9 * momentum)

        stores += [
            pltpu.make_async_copy(outer, no_h, local.at[1]),
            pltpu.make_async_copy(mom, nm_h, local.at[2]),
        ]
        for store in stores:
            store.start()

    loads[0].wait()

    @pl.loop(1, n)
    def _(k):
        src = lax.rem(me + k, n)
        remote(ig_s.at[src], ig_r.at[src], ig_send.at[src], ig_recv.at[src], src).wait_recv()

    @pl.loop(0, tokens // rows)
    def _(c):
        at = pl.ds(pl.multiple_of(c * rows, rows), rows)
        inverse = inv[at, 0:1]
        total = jnp.zeros((rows, feats), F32)
        for b in range(n):
            span = slice(b * feats, (b + 1) * feats)
            unit = hid[at, span].astype(F32) * inverse
            total += (ig_r[b, at, :].astype(F32) * gain[:, span]) * unit
        projection = jnp.sum(total, axis=1, keepdims=True) / width
        for b in range(n):
            span = slice(b * feats, (b + 1) * feats)
            unit = hid[at, span].astype(F32) * inverse
            scaled = ig_r[b, at, :].astype(F32) * gain[:, span]
            hg[at, span] = (
                res[at, span].astype(F32) + inverse * (scaled - unit * projection)
            ).astype(BF16)

    store = pltpu.make_async_copy(hg, hg_h, local.at[0])
    store.start()
    stores.append(store)

    def wg_dot(src):
        return lax.dot_general(
            nrm_r[src], vg_r[src], (((0,), (0,)), ((), ())), preferred_element_type=F32
        )

    def gg_sum(src):
        return jnp.sum(nrm_r[src].astype(F32) * ig_s[src].astype(F32), axis=0, keepdims=True)

    wg_acc[...] = wg_dot(me)
    gg_out[...] = gg_sum(me)

    @pl.loop(1, n)
    def _(k):
        src = lax.rem(me + k, n)
        remote(
            nrm_s.at[src], nrm_r.at[src], nrm_send.at[src], nrm_recv.at[src], src
        ).wait_recv()
        wg_acc[...] += wg_dot(src)
        gg_out[...] += gg_sum(src)

    wg_out[...] = wg_acc[...].astype(BF16)
    gg_out[...] = gg_out[...] / gain[:, cols(me)]

    vg_own(0, mirror).wait_send()
    for j in range(1, half):
        vg_own(j, near_peer(j)).wait_send()
        vg_forward(j).wait_send()
    for k in range(1, n):
        nrm_copy(lax.rem(me + k, n)).wait_send()
        ig_copy(lax.rem(me + k, n)).wait_send()
    if with_frag:
        for k in range(1, reps):
            fr_copy(k).wait_send()
            av_copy(k).wait_send()
    for store in stores:
        store.wait()


def outer_step(inner_frag, outer_frag, momentum):
    pseudo_grad = outer_frag - inner_frag
    average = lax.psum_scatter(
        pseudo_grad, "replica", scatter_dimension=1, tiled=True
    ) / lax.axis_size("replica")
    average = lax.all_gather(average.astype(BF16), "replica", axis=1, tiled=True).astype(F32)
    new_momentum = 0.9 * momentum + average
    return outer_frag - 0.7 * (average + 0.9 * new_momentum), new_momentum


def body(
    hidden_in, res_grad, value_grad, value_weight, norm_gain, inner_frag, outer_frag, momentum
):
    n, reps = lax.axis_size("fsdp"), lax.axis_size("replica")
    tokens, width = hidden_in.shape
    values = value_grad.shape[1]
    feats = value_weight.shape[1]
    frag_rows, frag_cols = outer_frag.shape
    with_frag = frag_rows % (16 * reps) == 0
    share = frag_rows // reps if with_frag else 16
    slots = reps if with_frag else 1
    frag_buffer = (frag_rows, frag_cols) if with_frag else (8, 128)
    half_buffer = (slots, share, frag_cols) if with_frag else (1, 16, 128)

    vmem = pl.BlockSpec(memory_space=pltpu.VMEM)
    anywhere = pl.BlockSpec(memory_space=pl.ANY)
    frag_out = frag_buffer
    dma = pltpu.SemaphoreType.DMA
    hidden_grad, weight_grad, gain_grad, new_outer, new_momentum = pl.pallas_call(
        functools.partial(kernel, n, reps, with_frag),
        out_shape=(
            jax.ShapeDtypeStruct((tokens, width), BF16),
            jax.ShapeDtypeStruct((feats, values), BF16),
            jax.ShapeDtypeStruct((1, feats), F32),
            jax.ShapeDtypeStruct(frag_out, F32),
            jax.ShapeDtypeStruct(frag_out, F32),
        ),
        in_specs=[vmem, anywhere, vmem, vmem, vmem, anywhere, anywhere, anywhere],
        out_specs=(anywhere, vmem, vmem, anywhere, anywhere),
        scratch_shapes=[
            pltpu.VMEM((tokens, 128), F32),
            pltpu.VMEM((n, tokens, feats), BF16),
            pltpu.VMEM((n, tokens, feats), BF16),
            pltpu.VMEM((n, tokens, values), BF16),
            pltpu.VMEM((n, tokens, feats), BF16),
            pltpu.VMEM((n, tokens, feats), BF16),
            pltpu.VMEM((feats, values), F32),
            pltpu.VMEM((tokens, width), BF16),
            pltpu.VMEM((tokens, width), BF16),
            pltpu.VMEM(frag_buffer, F32),
            pltpu.VMEM(frag_buffer, F32),
            pltpu.VMEM(frag_buffer, F32),
            pltpu.VMEM(half_buffer, BF16),
            pltpu.VMEM(half_buffer, BF16),
            pltpu.VMEM(half_buffer, BF16),
            dma((n,)), dma((n,)), dma((n,)), dma((n,)), dma((n,)), dma((n,)),
            dma((slots,)), dma((slots,)), dma((slots,)), dma((slots,)), dma((4,)),
        ],
        compiler_params=pltpu.CompilerParams(
            collective_id=0, has_side_effects=True, vmem_limit_bytes=40 * 2**20
        ),
    )(
        hidden_in, res_grad, value_grad, value_weight[0], norm_gain,
        inner_frag[0], outer_frag, momentum,
    )
    if not with_frag:
        new_outer, new_momentum = outer_step(inner_frag[0], outer_frag, momentum)
    return (hidden_grad, weight_grad[None], gain_grad, new_outer, new_momentum)


def solution(mesh):
    in_specs = (
        P(("replica", "fsdp"), None),
        P(("replica", "fsdp"), None),
        P(("replica", "fsdp"), None),
        P("replica", "fsdp", None),
        P("replica", None),
        P("replica", "fsdp", None),
        P("fsdp", None),
        P("fsdp", None),
    )
    out_specs = (
        P(("replica", "fsdp"), None),
        P("replica", "fsdp", None),
        P("replica", "fsdp"),
        P("fsdp", None),
        P("fsdp", None),
    )
    return jax.shard_map(body, mesh=mesh, in_specs=in_specs, out_specs=out_specs, check_vma=False)
```

```python
import functools

import jax
import jax.numpy as jnp
from jax import lax
from jax.experimental import pallas as pl
from jax.experimental.pallas import tpu as pltpu
from jax.sharding import PartitionSpec as P

MESH = pl.DeviceIdType.MESH
F32 = jnp.float32
BF16 = jnp.bfloat16
EPS = 1e-05


def kernel(
    n, reps, with_frag,
    hid_h, res_h, vg_h, w_h, gain_h, inner_h, outer_h, mom_h,
    hid, res, gain, inv, proj, ig_r, wg_out, gg_out, outer, mom,
    nrm_s, nrm_r, vg_r, ig_s, wg_acc, w, inner, ps, fr_r, av,
    vg_send, vg_recv, nrm_send, nrm_recv, ig_send, ig_recv,
    fr_send, fr_recv, av_send, av_recv, local,
):
    tokens, width = hid.shape
    feats = width // n
    half = n // 2
    me = lax.axis_index("fsdp")
    rep = lax.axis_index("replica")
    zrow, ycol = me // 2, lax.rem(me, 2)
    mirror = (half - 1 - zrow) * 2 + ycol
    base = (me // half) * half
    far = half - base
    mine, theirs = me - base, mirror - far

    def near_peer(j):
        return base + lax.rem(mine + j, half)

    def far_peer(j):
        return far + lax.rem(theirs + j, half)

    def cols(i):
        return pl.ds(pl.multiple_of(i * feats, feats), feats)

    def remote(src, dst, send, recv, dest, axis="fsdp"):
        return pltpu.make_async_remote_copy(
            src_ref=src, dst_ref=dst, send_sem=send, recv_sem=recv,
            device_id={axis: dest}, device_id_type=MESH,
        )

    load_vg = pltpu.make_async_copy(vg_h, vg_r.at[me], local.at[0])
    load_hid = pltpu.make_async_copy(hid_h, hid, local.at[1])
    load_gain = pltpu.make_async_copy(gain_h, gain, local.at[2])
    load_w = pltpu.make_async_copy(w_h, w, local.at[3])
    load_res = pltpu.make_async_copy(res_h, res, local.at[4])
    frag_loads = [
        pltpu.make_async_copy(inner_h, inner, local.at[5]),
        pltpu.make_async_copy(outer_h, outer, local.at[6]),
        pltpu.make_async_copy(mom_h, mom, local.at[7]),
    ] if with_frag else []
    for load in [load_vg, load_hid, load_gain, load_w, *frag_loads, load_res]:
        load.start()

    barrier = pltpu.get_barrier_semaphore()
    for k in range(1, n):
        pl.semaphore_signal(
            barrier, inc=1, device_id={"fsdp": lax.rem(me + k, n)}, device_id_type=MESH
        )
    if with_frag:
        for k in range(1, reps):
            pl.semaphore_signal(
                barrier, inc=1, device_id={"replica": lax.rem(rep + k, reps)}, device_id_type=MESH
            )
    load_vg.wait()
    pl.semaphore_wait(barrier, n - 1 + (reps - 1 if with_frag else 0))

    def vg_own(slot, dest):
        return remote(vg_r.at[me], vg_r.at[me], vg_send.at[slot], vg_recv.at[me], dest)

    def vg_forward(j):
        return remote(
            vg_r.at[mirror], vg_r.at[mirror], vg_send.at[half + j], vg_recv.at[mirror], near_peer(j)
        )

    def vg_wait(src):
        remote(
            vg_r.at[src], vg_r.at[src], vg_send.at[0], vg_recv.at[src], mirror
        ).wait_recv()

    vg_own(0, mirror).start()
    for j in range(1, half):
        vg_own(j, near_peer(j)).start()

    rows = 16
    tall = 32
    load_hid.wait()

    @pl.loop(0, tokens // rows)
    def _(c):
        at = pl.ds(pl.multiple_of(c * rows, rows), rows)
        total = jnp.zeros((rows, feats), F32)
        for b in range(n):
            x = hid[at, b * feats:(b + 1) * feats].astype(F32)
            total += x * x
        mean = jnp.sum(total, axis=1, keepdims=True) / width
        inv[at, :] = jnp.broadcast_to(lax.rsqrt(mean + EPS), (rows, 128))

    load_gain.wait()

    def norm_block(dest, out, slot):
        scale = gain[:, cols(dest)]

        @pl.loop(0, tokens // tall)
        def _(c):
            at = pl.ds(pl.multiple_of(c * tall, tall), tall)
            unit = hid[at, cols(dest)].astype(F32) * inv[at, 0:1]
            out[slot, at, :] = (unit * scale).astype(BF16)

    def nrm_copy(dest):
        return remote(
            nrm_s.at[dest], nrm_r.at[me], nrm_send.at[dest], nrm_recv.at[me], dest
        )

    @pl.loop(0, half)
    def _(j):
        dest = far_peer(j)
        norm_block(dest, nrm_s, dest)
        nrm_copy(dest).start()

    @pl.loop(1, half)
    def _(j):
        dest = near_peer(j)
        norm_block(dest, nrm_s, dest)
        nrm_copy(dest).start()

    norm_block(me, nrm_r, me)

    def fr_copy(k):
        dest = lax.rem(rep + k, reps)
        return remote(
            ps.at[dest], fr_r.at[rep], fr_send.at[dest], fr_recv.at[rep], dest, "replica"
        )

    def av_copy(k):
        dest = lax.rem(rep + k, reps)
        return remote(
            av.at[rep], av.at[rep], av_send.at[dest], av_recv.at[rep], dest, "replica"
        )

    if with_frag:
        share = ps.shape[1]
        steps = share // rows
        for load in frag_loads:
            load.wait()

        @pl.loop(0, reps * steps)
        def _(c):
            at = pl.ds(pl.multiple_of(c * rows, rows), rows)
            to = pl.ds(pl.multiple_of(lax.rem(c, steps) * rows, rows), rows)
            ps[c // steps, to, :] = (outer[at, :] - inner[at, :]).astype(BF16)

        for k in range(1, reps):
            fr_copy(k).start()

    vg_wait(mirror)
    for j in range(1, half):
        vg_forward(j).start()

    load_w.wait()

    def ig_dot(src):
        return lax.dot_general(
            vg_r[src], w[...], (((1,), (1,)), ((), ())), preferred_element_type=F32
        ).astype(BF16)

    def ig_copy(src):
        return remote(ig_s.at[src], ig_r.at[me], ig_send.at[src], ig_recv.at[me], src)

    ig_s[mirror] = ig_dot(mirror)
    ig_copy(mirror).start()

    @pl.loop(1, half)
    def _(j):
        src = near_peer(j)
        vg_wait(src)
        ig_s[src] = ig_dot(src)
        ig_copy(src).start()

    @pl.loop(1, half)
    def _(j):
        src = far_peer(j)
        vg_wait(src)
        ig_s[src] = ig_dot(src)
        ig_copy(src).start()

    own = ig_dot(me)
    ig_s[me] = own
    ig_r[me] = own

    if with_frag:
        for k in range(1, reps):
            src = lax.rem(rep + k, reps)
            remote(
                ps.at[src], fr_r.at[src], fr_send.at[src], fr_recv.at[src], src, "replica"
            ).wait_recv()
        fr_r[rep] = ps[rep]

        @pl.loop(0, steps)
        def _(c):
            at = pl.ds(pl.multiple_of(c * rows, rows), rows)
            total = fr_r[0, at, :].astype(F32)
            for r in range(1, reps):
                total += fr_r[r, at, :].astype(F32)
            av[rep, at, :] = (total / reps).astype(BF16)

        for k in range(1, reps):
            av_copy(k).start()
        for k in range(1, reps):
            src = lax.rem(rep + k, reps)
            remote(
                av.at[src], av.at[src], av_send.at[src], av_recv.at[src], src, "replica"
            ).wait_recv()

        @pl.loop(0, reps * steps)
        def _(c):
            at = pl.ds(pl.multiple_of(c * rows, rows), rows)
            to = pl.ds(pl.multiple_of(lax.rem(c, steps) * rows, rows), rows)
            average = av[c // steps, to, :].astype(F32)
            momentum = 0.9 * mom[at, :] + average
            mom[at, :] = momentum
            outer[at, :] = outer[at, :] - 0.7 * (average + 0.9 * momentum)

    def wg_dot(src):
        return lax.dot_general(
            nrm_r[src], vg_r[src], (((0,), (0,)), ((), ())), preferred_element_type=F32
        )

    def gg_sum(src):
        return jnp.sum(nrm_r[src].astype(F32) * ig_s[src].astype(F32), axis=0, keepdims=True)

    wg_acc[...] = wg_dot(me)
    gg_out[...] = gg_sum(me)

    def add_group(src):
        remote(
            nrm_s.at[src], nrm_r.at[src], nrm_send.at[src], nrm_recv.at[src], src
        ).wait_recv()
        wg_acc[...] += wg_dot(src)
        gg_out[...] += gg_sum(src)

    @pl.loop(1, half)
    def _(j):
        add_group(near_peer(j))

    @pl.loop(0, half)
    def _(j):
        add_group(far_peer(j))

    wg_out[...] = wg_acc[...].astype(BF16)
    gg_out[...] = gg_out[...] / gain[:, cols(me)]

    def project(src, first):
        scale = gain[:, cols(src)]

        @pl.loop(0, tokens // tall)
        def _(c):
            at = pl.ds(pl.multiple_of(c * tall, tall), tall)
            unit = hid[at, cols(src)].astype(F32) * inv[at, 0:1]
            term = (ig_r[src, at, :].astype(F32) * scale) * unit
            total = term[:, :128]
            for g in range(1, feats // 128):
                total += term[:, g * 128:(g + 1) * 128]
            proj[at, :] = total if first else proj[at, :] + total

    def add_block(src):
        remote(ig_s.at[src], ig_r.at[src], ig_send.at[src], ig_recv.at[src], src).wait_recv()
        project(src, False)

    project(me, True)

    @pl.loop(1, half)
    def _(j):
        add_block(near_peer(j))

    @pl.loop(0, half)
    def _(j):
        add_block(far_peer(j))

    vg_own(0, mirror).wait_send()
    for j in range(1, half):
        vg_own(j, near_peer(j)).wait_send()
        vg_forward(j).wait_send()
    for k in range(1, n):
        nrm_copy(lax.rem(me + k, n)).wait_send()
        ig_copy(lax.rem(me + k, n)).wait_send()
    if with_frag:
        for k in range(1, reps):
            fr_copy(k).wait_send()
            av_copy(k).wait_send()
    load_res.wait()


def finish(
    n, with_frag,
    hid, res, gain, inv, proj, ig, wg, gg, outer, mom,
    hg_h, wg_h, gg_h, no_h, nm_h,
    hg, sems, hg_sems,
):
    tokens, width = hid.shape
    feats = width // n
    tall = 32
    pairs = [(wg, wg_h), (gg, gg_h)] + ([(outer, no_h), (mom, nm_h)] if with_frag else [])
    stores = [pltpu.make_async_copy(a, b, sems.at[i]) for i, (a, b) in enumerate(pairs)]
    for store in stores:
        store.start()

    def hg_store(c):
        at = pl.ds(pl.multiple_of(c * tall, tall), tall)
        return pltpu.make_async_copy(hg.at[at], hg_h.at[at], hg_sems.at[c])

    @pl.loop(0, tokens // tall)
    def _(c):
        at = pl.ds(pl.multiple_of(c * tall, tall), tall)
        inverse = inv[at, 0:1]
        projection = jnp.sum(proj[at, :], axis=1, keepdims=True) / width
        for b in range(n):
            span = slice(b * feats, (b + 1) * feats)
            unit = hid[at, span].astype(F32) * inverse
            scaled = ig[b, at, :].astype(F32) * gain[:, span]
            hg[at, span] = (
                res[at, span].astype(F32) + inverse * (scaled - unit * projection)
            ).astype(BF16)
        hg_store(c).start()

    for c in range(tokens // tall):
        hg_store(c).wait()
    for store in stores:
        store.wait()


def outer_step(inner_frag, outer_frag, momentum):
    pseudo_grad = outer_frag - inner_frag
    average = lax.psum_scatter(
        pseudo_grad, "replica", scatter_dimension=1, tiled=True
    ) / lax.axis_size("replica")
    average = lax.all_gather(average.astype(BF16), "replica", axis=1, tiled=True).astype(F32)
    new_momentum = 0.9 * momentum + average
    return outer_frag - 0.7 * (average + 0.9 * new_momentum), new_momentum


def body(
    hidden_in, res_grad, value_grad, value_weight, norm_gain, inner_frag, outer_frag, momentum
):
    n, reps = lax.axis_size("fsdp"), lax.axis_size("replica")
    tokens, width = hidden_in.shape
    values = value_grad.shape[1]
    feats = value_weight.shape[1]
    frag_rows, frag_cols = outer_frag.shape
    with_frag = frag_rows % (16 * reps) == 0
    share = frag_rows // reps if with_frag else 16
    slots = reps if with_frag else 1
    frag_buffer = (frag_rows, frag_cols) if with_frag else (8, 128)
    half_buffer = (slots, share, frag_cols) if with_frag else (1, 16, 128)

    vmem = pl.BlockSpec(memory_space=pltpu.VMEM)
    hbm = pl.BlockSpec(memory_space=pltpu.HBM)
    dma = pltpu.SemaphoreType.DMA
    in_hbm = [
        pltpu.with_memory_space_constraint(x, pltpu.HBM)
        for x in (
            hidden_in, res_grad, value_grad, value_weight[0], norm_gain,
            inner_frag[0], outer_frag, momentum,
        )
    ]
    held = pl.pallas_call(
        functools.partial(kernel, n, reps, with_frag),
        out_shape=(
            jax.ShapeDtypeStruct((tokens, width), BF16),
            jax.ShapeDtypeStruct((tokens, width), BF16),
            jax.ShapeDtypeStruct((1, width), F32),
            jax.ShapeDtypeStruct((tokens, 128), F32),
            jax.ShapeDtypeStruct((tokens, 128), F32),
            jax.ShapeDtypeStruct((n, tokens, feats), BF16),
            jax.ShapeDtypeStruct((feats, values), BF16),
            jax.ShapeDtypeStruct((1, feats), F32),
            jax.ShapeDtypeStruct(frag_buffer, F32),
            jax.ShapeDtypeStruct(frag_buffer, F32),
        ),
        in_specs=[hbm] * 8,
        out_specs=(vmem,) * 10,
        scratch_shapes=[
            pltpu.VMEM((n, tokens, feats), BF16),
            pltpu.VMEM((n, tokens, feats), BF16),
            pltpu.VMEM((n, tokens, values), BF16),
            pltpu.VMEM((n, tokens, feats), BF16),
            pltpu.VMEM((feats, values), F32),
            pltpu.VMEM((feats, values), BF16),
            pltpu.VMEM(frag_buffer, F32),
            pltpu.VMEM(half_buffer, BF16),
            pltpu.VMEM(half_buffer, BF16),
            pltpu.VMEM(half_buffer, BF16),
            dma((n,)), dma((n,)), dma((n,)), dma((n,)), dma((n,)), dma((n,)),
            dma((slots,)), dma((slots,)), dma((slots,)), dma((slots,)), dma((8,)),
        ],
        compiler_params=pltpu.CompilerParams(
            collective_id=0, has_side_effects=True, vmem_limit_bytes=32 * 2**20
        ),
    )(*in_hbm)
    hidden_grad, weight_grad, gain_grad, new_outer, new_momentum = pl.pallas_call(
        functools.partial(finish, n, with_frag),
        out_shape=(
            jax.ShapeDtypeStruct((tokens, width), BF16),
            jax.ShapeDtypeStruct((feats, values), BF16),
            jax.ShapeDtypeStruct((1, feats), F32),
            jax.ShapeDtypeStruct(frag_buffer, F32),
            jax.ShapeDtypeStruct(frag_buffer, F32),
        ),
        in_specs=[vmem] * 10,
        out_specs=(hbm,) * 5,
        scratch_shapes=[pltpu.VMEM((tokens, width), BF16), dma((4,)), dma((tokens // 32,))],
        compiler_params=pltpu.CompilerParams(vmem_limit_bytes=32 * 2**20),
    )(*held)
    if not with_frag:
        new_outer, new_momentum = outer_step(inner_frag[0], outer_frag, momentum)
    return (hidden_grad, weight_grad[None], gain_grad, new_outer, new_momentum)


def solution(mesh):
    in_specs = (
        P(("replica", "fsdp"), None),
        P(("replica", "fsdp"), None),
        P(("replica", "fsdp"), None),
        P("replica", "fsdp", None),
        P("replica", None),
        P("replica", "fsdp", None),
        P("fsdp", None),
        P("fsdp", None),
    )
    out_specs = (
        P(("replica", "fsdp"), None),
        P("replica", "fsdp", None),
        P("replica", "fsdp"),
        P("fsdp", None),
        P("fsdp", None),
    )
    return jax.shard_map(body, mesh=mesh, in_specs=in_specs, out_specs=out_specs, check_vma=False)
```

```python
import functools

import jax
import jax.numpy as jnp
from jax import lax
from jax.experimental import pallas as pl
from jax.experimental.pallas import tpu as pltpu
from jax.sharding import PartitionSpec as P

MESH = pl.DeviceIdType.MESH
F32 = jnp.float32
BF16 = jnp.bfloat16
EPS = 1e-05


def kernel(
    n, reps, with_frag,
    hid_h, res_h, vg_h, w_h, gain_h, inner_h, outer_h, mom_h,
    hid, res, gain, inv, proj, ig_r, wg_out, gg_out, outer, mom,
    nrm_s, nrm_r, vg_r, ig_s, wg_acc, w, inner, ps, fr_r, av,
    vg_send, vg_recv, nrm_send, nrm_recv, ig_send, ig_recv,
    fr_send, fr_recv, av_send, av_recv, local,
):
    tokens, width = hid.shape
    feats = width // n
    half = n // 2
    me = lax.axis_index("fsdp")
    rep = lax.axis_index("replica")
    zrow, ycol = me // 2, lax.rem(me, 2)
    mirror = (half - 1 - zrow) * 2 + ycol
    base = (me // half) * half
    far = half - base
    mine, theirs = me - base, mirror - far

    def near_peer(j):
        return base + lax.rem(mine + j, half)

    def far_peer(j):
        return far + lax.rem(theirs + j, half)

    def near_source(j):
        return base + lax.rem(mine + half - j, half)

    def far_source(j):
        return far + lax.rem(theirs + half - j, half)

    def cols(i):
        return pl.ds(pl.multiple_of(i * feats, feats), feats)

    def remote(src, dst, send, recv, dest, axis="fsdp"):
        return pltpu.make_async_remote_copy(
            src_ref=src, dst_ref=dst, send_sem=send, recv_sem=recv,
            device_id={axis: dest}, device_id_type=MESH,
        )

    load_vg = pltpu.make_async_copy(vg_h, vg_r.at[me], local.at[0])
    load_hid = pltpu.make_async_copy(hid_h, hid, local.at[1])
    load_gain = pltpu.make_async_copy(gain_h, gain, local.at[2])
    load_w = pltpu.make_async_copy(w_h, w, local.at[3])
    load_res = pltpu.make_async_copy(res_h, res, local.at[4])
    frag_loads = [
        pltpu.make_async_copy(inner_h, inner, local.at[5]),
        pltpu.make_async_copy(outer_h, outer, local.at[6]),
        pltpu.make_async_copy(mom_h, mom, local.at[7]),
    ] if with_frag else []
    for load in [load_vg, load_hid, load_gain, load_w, *frag_loads, load_res]:
        load.start()

    barrier = pltpu.get_barrier_semaphore()
    for k in range(1, n):
        pl.semaphore_signal(
            barrier, inc=1, device_id={"fsdp": lax.rem(me + k, n)}, device_id_type=MESH
        )
    if with_frag:
        for k in range(1, reps):
            pl.semaphore_signal(
                barrier, inc=1, device_id={"replica": lax.rem(rep + k, reps)}, device_id_type=MESH
            )
    load_vg.wait()
    pl.semaphore_wait(barrier, n - 1 + (reps - 1 if with_frag else 0))

    def vg_own(slot, dest):
        return remote(vg_r.at[me], vg_r.at[me], vg_send.at[slot], vg_recv.at[me], dest)

    def vg_forward(j):
        return remote(
            vg_r.at[mirror], vg_r.at[mirror], vg_send.at[half + j], vg_recv.at[mirror], near_peer(j)
        )

    def vg_wait(src):
        remote(
            vg_r.at[src], vg_r.at[src], vg_send.at[0], vg_recv.at[src], mirror
        ).wait_recv()

    vg_own(0, mirror).start()
    for j in range(1, half):
        vg_own(j, near_peer(j)).start()

    rows = 16
    tall = 32
    load_hid.wait()

    @pl.loop(0, tokens // rows)
    def _(c):
        at = pl.ds(pl.multiple_of(c * rows, rows), rows)
        total = jnp.zeros((rows, feats), F32)
        for b in range(n):
            x = hid[at, b * feats:(b + 1) * feats].astype(F32)
            total += x * x
        mean = jnp.sum(total, axis=1, keepdims=True) / width
        inv[at, :] = jnp.broadcast_to(lax.rsqrt(mean + EPS), (rows, 128))

    load_gain.wait()

    def norm_block(dest, out, slot):
        scale = gain[:, cols(dest)]

        @pl.loop(0, tokens // tall)
        def _(c):
            at = pl.ds(pl.multiple_of(c * tall, tall), tall)
            unit = hid[at, cols(dest)].astype(F32) * inv[at, 0:1]
            out[slot, at, :] = (unit * scale).astype(BF16)

    def nrm_copy(dest):
        return remote(
            nrm_s.at[dest], nrm_r.at[me], nrm_send.at[dest], nrm_recv.at[me], dest
        )

    @pl.loop(0, half)
    def _(j):
        dest = far_peer(j)
        norm_block(dest, nrm_s, dest)
        nrm_copy(dest).start()

    @pl.loop(1, half)
    def _(j):
        dest = near_peer(j)
        norm_block(dest, nrm_s, dest)
        nrm_copy(dest).start()

    norm_block(me, nrm_r, me)

    def fr_copy(k):
        dest = lax.rem(rep + k, reps)
        return remote(
            ps.at[dest], fr_r.at[rep], fr_send.at[dest], fr_recv.at[rep], dest, "replica"
        )

    def av_copy(k):
        dest = lax.rem(rep + k, reps)
        return remote(
            av.at[rep], av.at[rep], av_send.at[dest], av_recv.at[rep], dest, "replica"
        )

    if with_frag:
        share = ps.shape[1]
        steps = share // rows
        for load in frag_loads:
            load.wait()

        @pl.loop(0, reps * steps)
        def _(c):
            at = pl.ds(pl.multiple_of(c * rows, rows), rows)
            to = pl.ds(pl.multiple_of(lax.rem(c, steps) * rows, rows), rows)
            ps[c // steps, to, :] = (outer[at, :] - inner[at, :]).astype(BF16)

        for k in range(1, reps):
            fr_copy(k).start()

    vg_wait(mirror)
    for j in range(1, half):
        vg_forward(j).start()

    load_w.wait()

    def ig_dot(src):
        return lax.dot_general(
            vg_r[src], w[...], (((1,), (1,)), ((), ())), preferred_element_type=F32
        ).astype(BF16)

    def ig_copy(src):
        return remote(ig_s.at[src], ig_r.at[me], ig_send.at[src], ig_recv.at[me], src)

    ig_s[mirror] = ig_dot(mirror)
    ig_copy(mirror).start()

    @pl.loop(1, half)
    def _(j):
        src = near_source(j)
        vg_wait(src)
        ig_s[src] = ig_dot(src)
        ig_copy(src).start()

    @pl.loop(1, half)
    def _(j):
        src = far_source(j)
        vg_wait(src)
        ig_s[src] = ig_dot(src)
        ig_copy(src).start()

    own = ig_dot(me)
    ig_s[me] = own
    ig_r[me] = own

    if with_frag:
        for k in range(1, reps):
            src = lax.rem(rep + k, reps)
            remote(
                ps.at[src], fr_r.at[src], fr_send.at[src], fr_recv.at[src], src, "replica"
            ).wait_recv()
        fr_r[rep] = ps[rep]

        @pl.loop(0, steps)
        def _(c):
            at = pl.ds(pl.multiple_of(c * rows, rows), rows)
            total = fr_r[0, at, :].astype(F32)
            for r in range(1, reps):
                total += fr_r[r, at, :].astype(F32)
            av[rep, at, :] = (total / reps).astype(BF16)

        for k in range(1, reps):
            av_copy(k).start()
        for k in range(1, reps):
            src = lax.rem(rep + k, reps)
            remote(
                av.at[src], av.at[src], av_send.at[src], av_recv.at[src], src, "replica"
            ).wait_recv()

        @pl.loop(0, reps * steps)
        def _(c):
            at = pl.ds(pl.multiple_of(c * rows, rows), rows)
            to = pl.ds(pl.multiple_of(lax.rem(c, steps) * rows, rows), rows)
            average = av[c // steps, to, :].astype(F32)
            momentum = 0.9 * mom[at, :] + average
            mom[at, :] = momentum
            outer[at, :] = outer[at, :] - 0.7 * (average + 0.9 * momentum)

    def wg_dot(src):
        return lax.dot_general(
            nrm_r[src], vg_r[src], (((0,), (0,)), ((), ())), preferred_element_type=F32
        )

    def gg_sum(src):
        return jnp.sum(nrm_r[src].astype(F32) * ig_s[src].astype(F32), axis=0, keepdims=True)

    def add_group(src):
        remote(
            nrm_s.at[src], nrm_r.at[src], nrm_send.at[src], nrm_recv.at[src], src
        ).wait_recv()
        wg_acc[...] += wg_dot(src)
        gg_out[...] += gg_sum(src)

    def project(src, first):
        scale = gain[:, cols(src)]

        @pl.loop(0, tokens // tall)
        def _(c):
            at = pl.ds(pl.multiple_of(c * tall, tall), tall)
            unit = hid[at, cols(src)].astype(F32) * inv[at, 0:1]
            term = (ig_r[src, at, :].astype(F32) * scale) * unit
            total = term[:, :128]
            for g in range(1, feats // 128):
                total += term[:, g * 128:(g + 1) * 128]
            proj[at, :] = total if first else proj[at, :] + total

    def add_block(src):
        remote(ig_s.at[src], ig_r.at[src], ig_send.at[src], ig_recv.at[src], src).wait_recv()
        project(src, False)

    wg_acc[...] = wg_dot(me)
    gg_out[...] = gg_sum(me)
    project(me, True)

    @pl.loop(1, half)
    def _(j):
        add_group(near_source(j))
        add_block(near_peer(j))

    @pl.loop(0, half)
    def _(j):
        add_group(far_source(j))
        add_block(far_peer(j))

    wg_out[...] = wg_acc[...].astype(BF16)
    gg_out[...] = gg_out[...] / gain[:, cols(me)]

    vg_own(0, mirror).wait_send()
    for j in range(1, half):
        vg_own(j, near_peer(j)).wait_send()
        vg_forward(j).wait_send()
    for k in range(1, n):
        nrm_copy(lax.rem(me + k, n)).wait_send()
        ig_copy(lax.rem(me + k, n)).wait_send()
    if with_frag:
        for k in range(1, reps):
            fr_copy(k).wait_send()
            av_copy(k).wait_send()
    load_res.wait()


def finish(
    n, with_frag,
    hid, res, gain, inv, proj, ig, wg, gg, outer, mom,
    hg_h, wg_h, gg_h, no_h, nm_h,
    hg, sems, hg_sems,
):
    tokens, width = hid.shape
    feats = width // n
    tall = 32
    pairs = [(wg, wg_h), (gg, gg_h)] + ([(outer, no_h), (mom, nm_h)] if with_frag else [])
    stores = [pltpu.make_async_copy(a, b, sems.at[i]) for i, (a, b) in enumerate(pairs)]
    for store in stores:
        store.start()

    def hg_store(c):
        at = pl.ds(pl.multiple_of(c * tall, tall), tall)
        return pltpu.make_async_copy(hg.at[at], hg_h.at[at], hg_sems.at[c])

    @pl.loop(0, tokens // tall)
    def _(c):
        at = pl.ds(pl.multiple_of(c * tall, tall), tall)
        inverse = inv[at, 0:1]
        projection = jnp.sum(proj[at, :], axis=1, keepdims=True) / width
        for b in range(n):
            span = slice(b * feats, (b + 1) * feats)
            unit = hid[at, span].astype(F32) * inverse
            scaled = ig[b, at, :].astype(F32) * gain[:, span]
            hg[at, span] = (
                res[at, span].astype(F32) + inverse * (scaled - unit * projection)
            ).astype(BF16)
        hg_store(c).start()

    for c in range(tokens // tall):
        hg_store(c).wait()
    for store in stores:
        store.wait()


def outer_step(inner_frag, outer_frag, momentum):
    pseudo_grad = outer_frag - inner_frag
    average = lax.psum_scatter(
        pseudo_grad, "replica", scatter_dimension=1, tiled=True
    ) / lax.axis_size("replica")
    average = lax.all_gather(average.astype(BF16), "replica", axis=1, tiled=True).astype(F32)
    new_momentum = 0.9 * momentum + average
    return outer_frag - 0.7 * (average + 0.9 * new_momentum), new_momentum


def body(
    hidden_in, res_grad, value_grad, value_weight, norm_gain, inner_frag, outer_frag, momentum
):
    n, reps = lax.axis_size("fsdp"), lax.axis_size("replica")
    tokens, width = hidden_in.shape
    values = value_grad.shape[1]
    feats = value_weight.shape[1]
    frag_rows, frag_cols = outer_frag.shape
    with_frag = frag_rows % (16 * reps) == 0
    share = frag_rows // reps if with_frag else 16
    slots = reps if with_frag else 1
    frag_buffer = (frag_rows, frag_cols) if with_frag else (8, 128)
    half_buffer = (slots, share, frag_cols) if with_frag else (1, 16, 128)

    vmem = pl.BlockSpec(memory_space=pltpu.VMEM)
    hbm = pl.BlockSpec(memory_space=pltpu.HBM)
    dma = pltpu.SemaphoreType.DMA
    in_hbm = [
        pltpu.with_memory_space_constraint(x, pltpu.HBM)
        for x in (
            hidden_in, res_grad, value_grad, value_weight[0], norm_gain,
            inner_frag[0], outer_frag, momentum,
        )
    ]
    held = pl.pallas_call(
        functools.partial(kernel, n, reps, with_frag),
        out_shape=(
            jax.ShapeDtypeStruct((tokens, width), BF16),
            jax.ShapeDtypeStruct((tokens, width), BF16),
            jax.ShapeDtypeStruct((1, width), F32),
            jax.ShapeDtypeStruct((tokens, 128), F32),
            jax.ShapeDtypeStruct((tokens, 128), F32),
            jax.ShapeDtypeStruct((n, tokens, feats), BF16),
            jax.ShapeDtypeStruct((feats, values), BF16),
            jax.ShapeDtypeStruct((1, feats), F32),
            jax.ShapeDtypeStruct(frag_buffer, F32),
            jax.ShapeDtypeStruct(frag_buffer, F32),
        ),
        in_specs=[hbm] * 8,
        out_specs=(vmem,) * 10,
        scratch_shapes=[
            pltpu.VMEM((n, tokens, feats), BF16),
            pltpu.VMEM((n, tokens, feats), BF16),
            pltpu.VMEM((n, tokens, values), BF16),
            pltpu.VMEM((n, tokens, feats), BF16),
            pltpu.VMEM((feats, values), F32),
            pltpu.VMEM((feats, values), BF16),
            pltpu.VMEM(frag_buffer, F32),
            pltpu.VMEM(half_buffer, BF16),
            pltpu.VMEM(half_buffer, BF16),
            pltpu.VMEM(half_buffer, BF16),
            dma((n,)), dma((n,)), dma((n,)), dma((n,)), dma((n,)), dma((n,)),
            dma((slots,)), dma((slots,)), dma((slots,)), dma((slots,)), dma((8,)),
        ],
        compiler_params=pltpu.CompilerParams(
            collective_id=0, has_side_effects=True, vmem_limit_bytes=32 * 2**20
        ),
    )(*in_hbm)
    hidden_grad, weight_grad, gain_grad, new_outer, new_momentum = pl.pallas_call(
        functools.partial(finish, n, with_frag),
        out_shape=(
            jax.ShapeDtypeStruct((tokens, width), BF16),
            jax.ShapeDtypeStruct((feats, values), BF16),
            jax.ShapeDtypeStruct((1, feats), F32),
            jax.ShapeDtypeStruct(frag_buffer, F32),
            jax.ShapeDtypeStruct(frag_buffer, F32),
        ),
        in_specs=[vmem] * 10,
        out_specs=(hbm,) * 5,
        scratch_shapes=[pltpu.VMEM((tokens, width), BF16), dma((4,)), dma((tokens // 32,))],
        compiler_params=pltpu.CompilerParams(vmem_limit_bytes=32 * 2**20),
    )(*held)
    if not with_frag:
        new_outer, new_momentum = outer_step(inner_frag[0], outer_frag, momentum)
    return (hidden_grad, weight_grad[None], gain_grad, new_outer, new_momentum)


def solution(mesh):
    in_specs = (
        P(("replica", "fsdp"), None),
        P(("replica", "fsdp"), None),
        P(("replica", "fsdp"), None),
        P("replica", "fsdp", None),
        P("replica", None),
        P("replica", "fsdp", None),
        P("fsdp", None),
        P("fsdp", None),
    )
    out_specs = (
        P(("replica", "fsdp"), None),
        P("replica", "fsdp", None),
        P("replica", "fsdp"),
        P("fsdp", None),
        P("fsdp", None),
    )
    return jax.shard_map(body, mesh=mesh, in_specs=in_specs, out_specs=out_specs, check_vma=False)
```

```python
import functools

import jax
import jax.numpy as jnp
from jax import lax
from jax.experimental import pallas as pl
from jax.experimental.pallas import tpu as pltpu
from jax.sharding import PartitionSpec as P

MESH = pl.DeviceIdType.MESH
F32 = jnp.float32
BF16 = jnp.bfloat16
EPS = 1e-05


def kernel(
    n, reps, with_frag,
    hid_h, res_h, vg_h, w_h, gain_h, inner_h, outer_h, mom_h,
    hid, res, gain, inv, proj, ig_r, wg_out, gg_out, outer, mom,
    nrm_s, nrm_r, vg_r, ig_s, wg_acc, w, inner, ps, fr_r, av,
    vg_send, vg_recv, nrm_send, nrm_recv, ig_send, ig_recv,
    fr_send, fr_recv, av_send, av_recv, local,
):
    tokens, width = hid.shape
    feats = width // n
    half = n // 2
    me = lax.axis_index("fsdp")
    rep = lax.axis_index("replica")
    zrow, ycol = me // 2, lax.rem(me, 2)
    mirror = (half - 1 - zrow) * 2 + ycol
    base = (me // half) * half
    far = half - base
    mine, theirs = me - base, mirror - far

    def near_peer(j):
        return base + lax.rem(mine + j, half)

    def far_peer(j):
        return far + lax.rem(theirs + j, half)

    def near_source(j):
        return base + lax.rem(mine + half - j, half)

    def far_source(j):
        return far + lax.rem(theirs + half - j, half)

    def cols(i):
        return pl.ds(pl.multiple_of(i * feats, feats), feats)

    def remote(src, dst, send, recv, dest, axis="fsdp"):
        return pltpu.make_async_remote_copy(
            src_ref=src, dst_ref=dst, send_sem=send, recv_sem=recv,
            device_id={axis: dest}, device_id_type=MESH,
        )

    load_vg = pltpu.make_async_copy(vg_h, vg_r.at[me], local.at[0])
    load_hid = pltpu.make_async_copy(hid_h, hid, local.at[1])
    load_gain = pltpu.make_async_copy(gain_h, gain, local.at[2])
    load_w = pltpu.make_async_copy(w_h, w, local.at[3])
    load_res = pltpu.make_async_copy(res_h, res, local.at[4])
    frag_loads = [
        pltpu.make_async_copy(inner_h, inner, local.at[5]),
        pltpu.make_async_copy(outer_h, outer, local.at[6]),
        pltpu.make_async_copy(mom_h, mom, local.at[7]),
    ] if with_frag else []
    for load in [load_vg, load_hid, load_gain, load_w, *frag_loads, load_res]:
        load.start()

    barrier = pltpu.get_barrier_semaphore()
    for k in range(1, n):
        pl.semaphore_signal(
            barrier, inc=1, device_id={"fsdp": lax.rem(me + k, n)}, device_id_type=MESH
        )
    if with_frag:
        for k in range(1, reps):
            pl.semaphore_signal(
                barrier, inc=1, device_id={"replica": lax.rem(rep + k, reps)}, device_id_type=MESH
            )
    load_vg.wait()
    pl.semaphore_wait(barrier, n - 1 + (reps - 1 if with_frag else 0))

    def vg_own(slot, dest):
        return remote(vg_r.at[me], vg_r.at[me], vg_send.at[slot], vg_recv.at[me], dest)

    def vg_forward(j):
        return remote(
            vg_r.at[mirror], vg_r.at[mirror], vg_send.at[half + j], vg_recv.at[mirror], near_peer(j)
        )

    def vg_wait(src):
        remote(
            vg_r.at[src], vg_r.at[src], vg_send.at[0], vg_recv.at[src], mirror
        ).wait_recv()

    vg_own(0, mirror).start()
    for j in range(1, half):
        vg_own(j, near_peer(j)).start()

    rows = 16
    tall = 32
    load_hid.wait()

    @pl.loop(0, tokens // rows)
    def _(c):
        at = pl.ds(pl.multiple_of(c * rows, rows), rows)
        total = jnp.zeros((rows, feats), F32)
        for b in range(n):
            x = hid[at, b * feats:(b + 1) * feats].astype(F32)
            total += x * x
        mean = jnp.sum(total, axis=1, keepdims=True) / width
        inv[at, :] = jnp.broadcast_to(lax.rsqrt(mean + EPS), (rows, 128))

    load_gain.wait()

    def norm_block(dest, out, slot):
        scale = gain[:, cols(dest)]

        @pl.loop(0, tokens // tall)
        def _(c):
            at = pl.ds(pl.multiple_of(c * tall, tall), tall)
            unit = hid[at, cols(dest)].astype(F32) * inv[at, 0:1]
            out[slot, at, :] = (unit * scale).astype(BF16)

    def nrm_copy(dest):
        return remote(
            nrm_s.at[dest], nrm_r.at[me], nrm_send.at[dest], nrm_recv.at[me], dest
        )

    def send_normed(dest):
        norm_block(dest, nrm_s, dest)
        nrm_copy(dest).start()

    send_normed(mirror)

    @pl.loop(1, half)
    def _(j):
        send_normed(near_peer(j))
        send_normed(far_peer(j))

    norm_block(me, nrm_r, me)

    def fr_copy(k):
        dest = lax.rem(rep + k, reps)
        return remote(
            ps.at[dest], fr_r.at[rep], fr_send.at[dest], fr_recv.at[rep], dest, "replica"
        )

    def av_copy(k):
        dest = lax.rem(rep + k, reps)
        return remote(
            av.at[rep], av.at[rep], av_send.at[dest], av_recv.at[rep], dest, "replica"
        )

    if with_frag:
        share = ps.shape[1]
        steps = share // rows
        for load in frag_loads:
            load.wait()

        @pl.loop(0, reps * steps)
        def _(c):
            at = pl.ds(pl.multiple_of(c * rows, rows), rows)
            to = pl.ds(pl.multiple_of(lax.rem(c, steps) * rows, rows), rows)
            ps[c // steps, to, :] = (outer[at, :] - inner[at, :]).astype(BF16)

        for k in range(1, reps):
            fr_copy(k).start()

    vg_wait(mirror)
    for j in range(1, half):
        vg_forward(j).start()

    load_w.wait()

    def ig_dot(src):
        return lax.dot_general(
            vg_r[src], w[...], (((1,), (1,)), ((), ())), preferred_element_type=F32
        ).astype(BF16)

    def ig_copy(src):
        return remote(ig_s.at[src], ig_r.at[me], ig_send.at[src], ig_recv.at[me], src)

    ig_s[mirror] = ig_dot(mirror)
    ig_copy(mirror).start()

    def send_block(src):
        vg_wait(src)
        ig_s[src] = ig_dot(src)
        ig_copy(src).start()

    @pl.loop(1, half)
    def _(j):
        send_block(near_source(j))
        send_block(far_source(j))

    own = ig_dot(me)
    ig_s[me] = own
    ig_r[me] = own

    if with_frag:
        for k in range(1, reps):
            src = lax.rem(rep + k, reps)
            remote(
                ps.at[src], fr_r.at[src], fr_send.at[src], fr_recv.at[src], src, "replica"
            ).wait_recv()
        fr_r[rep] = ps[rep]

        @pl.loop(0, steps)
        def _(c):
            at = pl.ds(pl.multiple_of(c * rows, rows), rows)
            total = fr_r[0, at, :].astype(F32)
            for r in range(1, reps):
                total += fr_r[r, at, :].astype(F32)
            av[rep, at, :] = (total / reps).astype(BF16)

        for k in range(1, reps):
            av_copy(k).start()
        for k in range(1, reps):
            src = lax.rem(rep + k, reps)
            remote(
                av.at[src], av.at[src], av_send.at[src], av_recv.at[src], src, "replica"
            ).wait_recv()

        @pl.loop(0, reps * steps)
        def _(c):
            at = pl.ds(pl.multiple_of(c * rows, rows), rows)
            to = pl.ds(pl.multiple_of(lax.rem(c, steps) * rows, rows), rows)
            average = av[c // steps, to, :].astype(F32)
            momentum = 0.9 * mom[at, :] + average
            mom[at, :] = momentum
            outer[at, :] = outer[at, :] - 0.7 * (average + 0.9 * momentum)

    def wg_dot(src):
        return lax.dot_general(
            nrm_r[src], vg_r[src], (((0,), (0,)), ((), ())), preferred_element_type=F32
        )

    def gg_sum(src):
        return jnp.sum(nrm_r[src].astype(F32) * ig_s[src].astype(F32), axis=0, keepdims=True)

    def add_group(src):
        remote(
            nrm_s.at[src], nrm_r.at[src], nrm_send.at[src], nrm_recv.at[src], src
        ).wait_recv()
        wg_acc[...] += wg_dot(src)
        gg_out[...] += gg_sum(src)

    def project(src, first):
        scale = gain[:, cols(src)]

        @pl.loop(0, tokens // tall)
        def _(c):
            at = pl.ds(pl.multiple_of(c * tall, tall), tall)
            unit = hid[at, cols(src)].astype(F32) * inv[at, 0:1]
            term = (ig_r[src, at, :].astype(F32) * scale) * unit
            total = term[:, :128]
            for g in range(1, feats // 128):
                total += term[:, g * 128:(g + 1) * 128]
            proj[at, :] = total if first else proj[at, :] + total

    def add_block(src):
        remote(ig_s.at[src], ig_r.at[src], ig_send.at[src], ig_recv.at[src], src).wait_recv()
        project(src, False)

    wg_acc[...] = wg_dot(me)
    gg_out[...] = gg_sum(me)
    project(me, True)

    @pl.loop(1, half)
    def _(j):
        add_group(near_source(j))
        add_block(near_peer(j))

    @pl.loop(0, half)
    def _(j):
        add_group(far_source(j))
        add_block(far_peer(j))

    wg_out[...] = wg_acc[...].astype(BF16)
    gg_out[...] = gg_out[...] / gain[:, cols(me)]

    vg_own(0, mirror).wait_send()
    for j in range(1, half):
        vg_own(j, near_peer(j)).wait_send()
        vg_forward(j).wait_send()
    for k in range(1, n):
        nrm_copy(lax.rem(me + k, n)).wait_send()
        ig_copy(lax.rem(me + k, n)).wait_send()
    if with_frag:
        for k in range(1, reps):
            fr_copy(k).wait_send()
            av_copy(k).wait_send()
    load_res.wait()


def finish(
    n, with_frag,
    hid, res, gain, inv, proj, ig, wg, gg, outer, mom,
    hg_h, wg_h, gg_h, no_h, nm_h,
    hg, sems, hg_sems,
):
    tokens, width = hid.shape
    feats = width // n
    tall = 32
    pairs = [(wg, wg_h), (gg, gg_h)] + ([(outer, no_h), (mom, nm_h)] if with_frag else [])
    stores = [pltpu.make_async_copy(a, b, sems.at[i]) for i, (a, b) in enumerate(pairs)]
    for store in stores:
        store.start()

    def hg_store(c):
        at = pl.ds(pl.multiple_of(c * tall, tall), tall)
        return pltpu.make_async_copy(hg.at[at], hg_h.at[at], hg_sems.at[c])

    @pl.loop(0, tokens // tall)
    def _(c):
        at = pl.ds(pl.multiple_of(c * tall, tall), tall)
        inverse = inv[at, 0:1]
        projection = jnp.sum(proj[at, :], axis=1, keepdims=True) / width
        for b in range(n):
            span = slice(b * feats, (b + 1) * feats)
            unit = hid[at, span].astype(F32) * inverse
            scaled = ig[b, at, :].astype(F32) * gain[:, span]
            hg[at, span] = (
                res[at, span].astype(F32) + inverse * (scaled - unit * projection)
            ).astype(BF16)
        hg_store(c).start()

    for c in range(tokens // tall):
        hg_store(c).wait()
    for store in stores:
        store.wait()


def outer_step(inner_frag, outer_frag, momentum):
    pseudo_grad = outer_frag - inner_frag
    average = lax.psum_scatter(
        pseudo_grad, "replica", scatter_dimension=1, tiled=True
    ) / lax.axis_size("replica")
    average = lax.all_gather(average.astype(BF16), "replica", axis=1, tiled=True).astype(F32)
    new_momentum = 0.9 * momentum + average
    return outer_frag - 0.7 * (average + 0.9 * new_momentum), new_momentum


def body(
    hidden_in, res_grad, value_grad, value_weight, norm_gain, inner_frag, outer_frag, momentum
):
    n, reps = lax.axis_size("fsdp"), lax.axis_size("replica")
    tokens, width = hidden_in.shape
    values = value_grad.shape[1]
    feats = value_weight.shape[1]
    frag_rows, frag_cols = outer_frag.shape
    with_frag = frag_rows % (16 * reps) == 0
    share = frag_rows // reps if with_frag else 16
    slots = reps if with_frag else 1
    frag_buffer = (frag_rows, frag_cols) if with_frag else (8, 128)
    half_buffer = (slots, share, frag_cols) if with_frag else (1, 16, 128)

    vmem = pl.BlockSpec(memory_space=pltpu.VMEM)
    hbm = pl.BlockSpec(memory_space=pltpu.HBM)
    dma = pltpu.SemaphoreType.DMA
    in_hbm = [
        pltpu.with_memory_space_constraint(x, pltpu.HBM)
        for x in (
            hidden_in, res_grad, value_grad, value_weight[0], norm_gain,
            inner_frag[0], outer_frag, momentum,
        )
    ]
    held = pl.pallas_call(
        functools.partial(kernel, n, reps, with_frag),
        out_shape=(
            jax.ShapeDtypeStruct((tokens, width), BF16),
            jax.ShapeDtypeStruct((tokens, width), BF16),
            jax.ShapeDtypeStruct((1, width), F32),
            jax.ShapeDtypeStruct((tokens, 128), F32),
            jax.ShapeDtypeStruct((tokens, 128), F32),
            jax.ShapeDtypeStruct((n, tokens, feats), BF16),
            jax.ShapeDtypeStruct((feats, values), BF16),
            jax.ShapeDtypeStruct((1, feats), F32),
            jax.ShapeDtypeStruct(frag_buffer, F32),
            jax.ShapeDtypeStruct(frag_buffer, F32),
        ),
        in_specs=[hbm] * 8,
        out_specs=(vmem,) * 10,
        scratch_shapes=[
            pltpu.VMEM((n, tokens, feats), BF16),
            pltpu.VMEM((n, tokens, feats), BF16),
            pltpu.VMEM((n, tokens, values), BF16),
            pltpu.VMEM((n, tokens, feats), BF16),
            pltpu.VMEM((feats, values), F32),
            pltpu.VMEM((feats, values), BF16),
            pltpu.VMEM(frag_buffer, F32),
            pltpu.VMEM(half_buffer, BF16),
            pltpu.VMEM(half_buffer, BF16),
            pltpu.VMEM(half_buffer, BF16),
            dma((n,)), dma((n,)), dma((n,)), dma((n,)), dma((n,)), dma((n,)),
            dma((slots,)), dma((slots,)), dma((slots,)), dma((slots,)), dma((8,)),
        ],
        compiler_params=pltpu.CompilerParams(
            collective_id=0, has_side_effects=True, vmem_limit_bytes=32 * 2**20
        ),
    )(*in_hbm)
    hidden_grad, weight_grad, gain_grad, new_outer, new_momentum = pl.pallas_call(
        functools.partial(finish, n, with_frag),
        out_shape=(
            jax.ShapeDtypeStruct((tokens, width), BF16),
            jax.ShapeDtypeStruct((feats, values), BF16),
            jax.ShapeDtypeStruct((1, feats), F32),
            jax.ShapeDtypeStruct(frag_buffer, F32),
            jax.ShapeDtypeStruct(frag_buffer, F32),
        ),
        in_specs=[vmem] * 10,
        out_specs=(hbm,) * 5,
        scratch_shapes=[pltpu.VMEM((tokens, width), BF16), dma((4,)), dma((tokens // 32,))],
        compiler_params=pltpu.CompilerParams(vmem_limit_bytes=32 * 2**20),
    )(*held)
    if not with_frag:
        new_outer, new_momentum = outer_step(inner_frag[0], outer_frag, momentum)
    return (hidden_grad, weight_grad[None], gain_grad, new_outer, new_momentum)


def solution(mesh):
    in_specs = (
        P(("replica", "fsdp"), None),
        P(("replica", "fsdp"), None),
        P(("replica", "fsdp"), None),
        P("replica", "fsdp", None),
        P("replica", None),
        P("replica", "fsdp", None),
        P("fsdp", None),
        P("fsdp", None),
    )
    out_specs = (
        P(("replica", "fsdp"), None),
        P("replica", "fsdp", None),
        P("replica", "fsdp"),
        P("fsdp", None),
        P("fsdp", None),
    )
    return jax.shard_map(body, mesh=mesh, in_specs=in_specs, out_specs=out_specs, check_vma=False)
```
